32 devices in a mesh: dp: 8 (over z, y), fsdp: 4 (over x, core).
Axes of the slice: x: 2, y: 2, z: 4, core: 2. Of those that a mesh axis runs over, the one named last changes fastest.
Arguments:
- drafts: bfloat16 [1024, 2048], P(('dp', 'fsdp')), may hold values from -6 to 6
- cache: bfloat16 [32, 2, 768, 1024], P(('dp', 'fsdp')), may hold values from -7 to 7
- cache_len: int32 [32], P(('dp', 'fsdp')), may hold values from 2 to 768, as said below
- parents: int32 [32, 32], P(('dp', 'fsdp')), may hold values from 0 to 30, as said below
- accepted: int32 [32], P(('dp', 'fsdp')), may hold values from 0 to 31
- order: int32 [32], replicated, may hold values from 0 to 31, each once
- attn_gain: float32 [2048], replicated, may hold values from 0.5 to 1.5
- w_qkv: bfloat16 [2048, 3072], P(None, 'fsdp'), may hold values from -0.125 to 0.125
- qkv_bias: float32 [3072], replicated, may hold values from -5 to 5
- w_out: bfloat16 [1024, 2048], P(None, 'fsdp'), may hold values from -0.1875 to 0.1875
- moe_gain: float32 [2048], replicated, may hold values from 0.5 to 1.5
- router: bfloat16 [2048, 8], replicated, may hold values from -0.125 to 0.125
- expert_ids: int32 [1024, 4], P('dp'), may hold values from 0 to 7, all different within a row; in each aligned block of 128 rows (0 to 127, 128 to 255, ...) at most 128 rows name the same one
- w_gate_up: bfloat16 [8, 2, 2048, 1408], P('dp', None, None, 'fsdp'), may hold values from -0.125 to 0.125
- w_down: bfloat16 [8, 1408, 2048], P('dp', 'fsdp'), may hold values from -0.15625 to 0.15625
Outputs:
- layer_out: bfloat16 [1024, 2048], P(('dp', 'fsdp'))
- appended: bfloat16 [32, 2, 32, 1024], P(('dp', 'fsdp'))
- last_state: bfloat16 [32, 2048], replicated
The draws below stay inside these ranges and needn't reach their ends.
Inputs may be any that keep to these rules, and one draw needn't show every extreme that they name: `cache_len`: some request has all 768 slots valid. parents[r, 0] is 0, and parents[r, i] < i for every node i >= 1. `expert_ids`: each row names 4 different experts; among the 128 rows of one index of dp no expert is named more than 128 times, and in some of them one expert exactly 128 times.
All inputs are finite; a program needn't handle non-finite values.
Results may differ from the reference program's by a relative error of at most 0.014.
Values may be sent and summed in bfloat16 or wider, within the bound.
A program may use at most 128 MiB of HBM per device.

```python
import math
import jax
import jax.numpy as jnp
import numpy as np
from jax import lax

D = 2048
HEADS = 8
HD = 128
FFE = 1408
TOPK = 4
TREE = 32
REQ_DEV = 1
CACHE = 768
EXPERTS = 8
REQUESTS = 32
TOKENS = 1024
CAP = 128
N_DP = 8
N_FSDP = 4


def draw_qkv_bias(key, part):
    noise = jnp.clip(jax.random.normal(jax.random.fold_in(key, 3), (HEADS, 3, HD), jnp.float32), -4.0, 4.0)
    bias = 0.5 * noise
    return bias.reshape(HEADS * 3 * HD).astype(jnp.float32)


def draw_cache(key, part):
    shape = (REQUESTS, 2, CACHE, HEADS, HD)
    values = jnp.clip(jax.random.normal(jax.random.fold_in(key, 13), shape, jnp.float32), -4.0, 4.0)
    return values.reshape(REQUESTS, 2, CACHE, HEADS * HD).astype(jnp.bfloat16)


def draw_cache_len(key, part):
    lengths = jax.random.randint(jax.random.fold_in(key, 21), (REQUESTS,), 2, CACHE + 1)
    longest = jax.random.randint(jax.random.fold_in(key, 22), (), 0, REQUESTS)
    return jnp.where(jnp.arange(REQUESTS) == longest, CACHE, lengths).astype(jnp.int32)


def draw_parents(key, part):
    index = jnp.arange(TREE, dtype=jnp.int32)
    anywhere = jax.random.randint(jax.random.fold_in(key, 31), (REQUESTS, TREE), 0, jnp.maximum(index, 1))
    chained = jax.random.randint(jax.random.fold_in(key, 32), (REQUESTS, TREE), 0, 2)
    return jnp.where(chained == 1, jnp.maximum(index - 1, 0), anywhere).astype(jnp.int32)


def set_ends(values, own_key, low, largest):
    longest = values.shape.index(max(values.shape))
    spots = []
    for shift in (0, 1):
        where = [jax.random.randint(jax.random.fold_in(own_key, axis), (), 0, length) for axis, length in enumerate(values.shape)]
        where[longest] = (where[longest] + shift) % values.shape[longest]
        spots.append(tuple(where))
    return values.at[spots[0]].set(low).at[spots[1]].set(largest)


def level_of(stream_key, shape, pieces, smallest, high):
    def one(dim, parts):
        draws = jax.random.uniform(jax.random.fold_in(jax.random.fold_in(stream_key, 6), dim), (parts,), jnp.float32, smallest / len(pieces), high / len(pieces))
        return jnp.repeat(jnp.exp(draws), shape[dim] // parts).reshape((-1,) + (1,) * (len(shape) - dim - 1))

    level = one(*pieces[0])
    for cut in pieces[1:]:
        level = level * one(*cut)
    return level


def assign_block(own_key, own, number, rows, count, top, bound, slope):
    ranking = jax.random.permutation(own_key, count)
    packed, usual = shares(count, rows * top, bound, slope, True), shares(count, rows * top, bound, slope, False)
    places = jnp.arange(count)

    def named(sizes, offset_by):
        used = int((sizes > 0).sum())
        fixed = max(1, used // 4)
        passed = fixed + (places - fixed + offset_by * (used - fixed)) % max(1, count - fixed)
        return jnp.zeros((count,), jnp.int32).at[ranking[jnp.where(places < fixed, places, passed)]].set(jnp.asarray(sizes, jnp.int32))

    sizes = jnp.where(number % 4 == 0, named(packed, number // 4), named(usual, number - number // 4 - 1))
    mixed = jax.random.permutation(jax.random.fold_in(own, 3), count)
    source_of, receiver = mixed[0:count // 2 * 2:2], mixed[1:count // 2 * 2:2]
    slack = jnp.minimum(sizes[source_of] - 1, bound - sizes[receiver]) // 2
    slack = jnp.where((source_of == ranking[0]) | (receiver == ranking[0]) | (sizes[receiver] == 0), 0, jnp.maximum(slack, 0))
    passed = jax.random.randint(jax.random.fold_in(own, 4), (count // 2,), 0, 1 << 20) % (slack + 1)
    sizes = sizes.at[source_of].add(-passed).at[receiver].add(passed)
    labels = jnp.searchsorted(jnp.cumsum(sizes), jnp.arange(rows * top), side="right").astype(jnp.int32)
    grid = labels.reshape(top, rows).T
    grid = grid[jax.random.permutation(jax.random.fold_in(own, 1), rows)]
    offset_by = jax.random.randint(jax.random.fold_in(own, 2), (rows, 1), 0, top)
    return jnp.take_along_axis(grid, (jnp.arange(top)[None, :] + offset_by) % top, axis=1)


def shares(number_of, total, bound, slope, full):
    loads = [(1 << 20) // math.isqrt(standing ** slope) + 1 for standing in range(1, number_of + 1)]
    largest = bound if full else min(bound, max(-(-total // number_of), total * loads[0] // sum(loads)))
    least = 1 if total - largest >= number_of - 1 else 0
    holding, rest = [largest] + [least] * (number_of - 1), total - largest - least * (number_of - 1)
    while rest > 0:
        movable = [i for i in range(1, number_of) if holding[i] < largest] or [i for i in range(1, number_of) if holding[i] < bound]
        whole, left = sum([loads[i] for i in movable]), rest
        for i in movable:
            addition = min(bound - holding[i], max(1, left * loads[i] // whole), rest)
            holding[i] = holding[i] + addition
            rest = rest - addition
    return np.array(holding)


def gaussian(rng, extent, width, most, cuts=(), kind=jnp.bfloat16):
    level = level_of(rng, extent, cuts, -0.22, 0.18) if cuts else 1.0
    entries = jax.random.normal(rng, extent, jnp.float32) * width * level
    return jnp.minimum(jnp.maximum(entries, -most), most).astype(kind)


def setup_inputs(seed: int = 0) -> dict:
    arg_keys = jax.random.split(jax.random.key(seed), 16)
    drafts = gaussian(arg_keys[0], (TOKENS, D), 1.0, 6.0, ((0, 32),))
    cache = draw_cache(jax.random.fold_in(arg_keys[15], 71), 0)
    cache_len = draw_cache_len(jax.random.fold_in(arg_keys[15], 71), 0)
    parents = draw_parents(jax.random.fold_in(arg_keys[15], 71), 0)
    accepted = set_ends(jax.random.randint(arg_keys[4], (REQUESTS,), 0, TREE), jax.random.fold_in(arg_keys[4], 1), 0, TREE - 1).astype(jnp.int32)
    order = jax.random.permutation(arg_keys[5], REQUESTS).astype(jnp.int32)
    attn_gain = jnp.clip(1.0 + 0.1 * jax.random.normal(arg_keys[6], (D,), jnp.float32), 0.5, 1.5)
    w_qkv = gaussian(arg_keys[7], (D, HEADS * 3 * HD), D ** -0.5, 0.125, ((1, 4),))
    qkv_bias = draw_qkv_bias(jax.random.fold_in(arg_keys[15], 71), 0)
    w_out = gaussian(arg_keys[9], (HEADS * HD, D), (HEADS * HD) ** -0.5, 0.1875, ((1, 4),))
    moe_gain = jnp.clip(1.0 + 0.1 * jax.random.normal(arg_keys[10], (D,), jnp.float32), 0.5, 1.5)
    router = gaussian(arg_keys[11], (D, EXPERTS), D ** -0.5, 0.125)
    expert_ids_keys = jax.random.split(jax.random.fold_in(arg_keys[12], 1), TOKENS // (N_FSDP * REQ_DEV * TREE))
    expert_ids_turns = jax.random.permutation(jax.random.fold_in(arg_keys[12], 3), TOKENS // (N_FSDP * REQ_DEV * TREE))
    expert_ids = jax.vmap(lambda own, number: assign_block(jax.random.fold_in(arg_keys[12], 2), own, number, N_FSDP * REQ_DEV * TREE, EXPERTS, TOPK, CAP, 2))(expert_ids_keys, expert_ids_turns).reshape((TOKENS, TOPK))
    w_gate_up = gaussian(arg_keys[13], (EXPERTS, 2, D, FFE), D ** -0.5, 0.125, ((0, 8), (3, 4)))
    w_down = gaussian(arg_keys[14], (EXPERTS, FFE, D), FFE ** -0.5, 0.15625, ((0, 8), (1, 4)))
    return dict(drafts=drafts, cache=cache, cache_len=cache_len, parents=parents, accepted=accepted, order=order, attn_gain=attn_gain, w_qkv=w_qkv, qkv_bias=qkv_bias, w_out=w_out, moe_gain=moe_gain, router=router, expert_ids=expert_ids, w_gate_up=w_gate_up, w_down=w_down)


EPS = 1e-06

def scaled_norm(values, gain):
    wide = values.astype(jnp.float32)
    factor = lax.rsqrt(lax.optimization_barrier(jnp.mean(wide * wide, axis=-1, keepdims=True)) + EPS)
    return (wide * factor * gain).astype(jnp.bfloat16)

def ancestors(parent_row):
    count = parent_row.shape[0]
    index = jnp.arange(count, dtype=jnp.int32)
    links = (index[:, None] == index[None, :]) | (parent_row[:, None] == index[None, :])
    closure = links.astype(jnp.float32)
    for level in range((count - 1).bit_length()):
        closure = jnp.minimum(jnp.dot(closure, closure, precision=lax.Precision.HIGHEST), 1.0)
    return closure

def attend(block, cache_block, valid_slots, closure):
    query = block[:, :, 0].astype(jnp.float32)
    tree_keys = block[:, :, 1].astype(jnp.float32)
    tree_values = block[:, :, 2].astype(jnp.float32)
    slots = cache_block.shape[1]
    cache_keys = cache_block[0].reshape(slots, HEADS, HD).astype(jnp.float32)
    cache_values = cache_block[1].reshape(slots, HEADS, HD).astype(jnp.float32)
    factor = 1.0 / math.sqrt(HD)
    cache_scores = jnp.einsum('thd,chd->htc', query, cache_keys) * factor
    position = jnp.arange(slots, dtype=jnp.int32)
    cache_scores = jnp.where(position[None, None, :] < valid_slots, cache_scores, -1e+30)
    tree_scores = jnp.einsum('thd,shd->hts', query, tree_keys) * factor
    tree_scores = jnp.where(closure[None] > 0.5, tree_scores, -1e+30)
    top = jnp.maximum(lax.optimization_barrier(jnp.max(cache_scores, axis=-1)), lax.optimization_barrier(jnp.max(tree_scores, axis=-1)))[..., None]
    cache_exp = jnp.exp(cache_scores - top)
    tree_exp = jnp.exp(tree_scores - top)
    total = lax.optimization_barrier(jnp.sum(cache_exp, axis=-1, keepdims=True)) + lax.optimization_barrier(jnp.sum(tree_exp, axis=-1, keepdims=True))
    cache_weights = (cache_exp / total).astype(jnp.bfloat16).astype(jnp.float32)
    tree_weights = (tree_exp / total).astype(jnp.bfloat16).astype(jnp.float32)
    mixed = jnp.einsum('htc,chd->thd', cache_weights, cache_values)
    mixed = mixed + jnp.einsum('hts,shd->thd', tree_weights, tree_values)
    return mixed.astype(jnp.bfloat16).reshape(block.shape[0], HEADS * HD)

def compact(closure, accepted_node, block):
    count = closure.shape[0]
    depth = lax.optimization_barrier(jnp.sum(closure, axis=1)) - 1.0
    on_path = lax.dynamic_index_in_dim(closure, accepted_node, 0, keepdims=False)
    levels = jnp.arange(count, dtype=jnp.int32).astype(jnp.float32)
    select = (on_path[None, :] * (depth[None, :] == levels[:, None]).astype(jnp.float32)).astype(jnp.bfloat16)
    tree_keys = block[:, :, 1].reshape(count, HEADS * HD)
    tree_values = block[:, :, 2].reshape(count, HEADS * HD)
    kept_keys = jnp.dot(select, tree_keys, preferred_element_type=jnp.float32).astype(jnp.bfloat16)
    kept_values = jnp.dot(select, tree_values, preferred_element_type=jnp.float32).astype(jnp.bfloat16)
    return jnp.stack([kept_keys, kept_values])

def slots_of(group_ids, experts):
    flat = group_ids.reshape(-1)
    onehot = (flat[:, None] == jnp.arange(experts, dtype=jnp.int32)[None, :]).astype(jnp.int32)
    earlier = jnp.cumsum(onehot, axis=0) - onehot
    return lax.optimization_barrier(jnp.sum(earlier * onehot, axis=1)).astype(jnp.int32)

def reference(drafts, cache, cache_len, parents, accepted, order, attn_gain, w_qkv, qkv_bias, w_out, moe_gain, router, expert_ids, w_gate_up, w_down):
    normed = scaled_norm(drafts, attn_gain)
    qkv = (jnp.dot(normed, w_qkv, preferred_element_type=jnp.float32) + qkv_bias).astype(jnp.bfloat16)
    qkv = qkv.reshape(REQUESTS, TREE, HEADS, 3, HD)

    def per_request(inputs):
        block, cache_block, valid_slots, parent_row, accepted_node = inputs
        closure = ancestors(parent_row)
        return (attend(block, cache_block, valid_slots, closure), compact(closure, accepted_node, block))
    attn, appended = lax.map(per_request, (qkv, cache, cache_len, parents, accepted))
    attn = attn.reshape(TOKENS, HEADS * HD)
    projected = jnp.dot(attn, w_out, preferred_element_type=jnp.float32)
    resid = (drafts.astype(jnp.float32) + projected).astype(jnp.bfloat16)
    moe_input = scaled_norm(resid, moe_gain)
    logits = jnp.dot(moe_input, router, preferred_element_type=jnp.float32)
    gates = jax.nn.sigmoid(jnp.take_along_axis(logits, expert_ids, axis=1))
    group = N_FSDP * REQ_DEV * TREE
    slots = jax.vmap(lambda rows: slots_of(rows, EXPERTS))(expert_ids.reshape(N_DP, group * TOPK))
    flat_column = (jnp.arange(N_DP, dtype=jnp.int32)[:, None] * CAP + slots).reshape(-1)
    flat_expert = expert_ids.reshape(-1)
    token_index = jnp.arange(TOKENS * TOPK, dtype=jnp.int32) // TOPK
    table = jnp.full((EXPERTS, N_DP * CAP), TOKENS, jnp.int32).at[flat_expert, flat_column].set(token_index)
    padded = jnp.concatenate([moe_input, jnp.zeros((1, D), jnp.bfloat16)], axis=0)
    quarter = FFE // N_FSDP

    def expert_run(inputs):
        row_index, gate_up, down = inputs
        chosen = padded[row_index]
        gate = jnp.dot(chosen, gate_up[0], preferred_element_type=jnp.float32)
        upward = jnp.dot(chosen, gate_up[1], preferred_element_type=jnp.float32)
        hidden = (jax.nn.silu(gate) * upward).astype(jnp.bfloat16)
        total = jnp.zeros((chosen.shape[0], D), jnp.float32)
        for share in range(N_FSDP):
            part = jnp.dot(hidden[:, share * quarter:(share + 1) * quarter], down[share * quarter:(share + 1) * quarter], preferred_element_type=jnp.float32)
            total = total + lax.optimization_barrier(part.astype(jnp.bfloat16)).astype(jnp.float32)
        return total
    outputs = lax.map(expert_run, (table, w_gate_up, w_down)).reshape(EXPERTS * N_DP * CAP, D)
    picked = outputs[flat_expert * (N_DP * CAP) + flat_column].reshape(TOKENS, TOPK, D)
    moe = lax.optimization_barrier(jnp.sum(picked * gates[:, :, None], axis=1))
    layer_out = (resid.astype(jnp.float32) + moe).astype(jnp.bfloat16)
    final_rows = layer_out.reshape(REQUESTS, TREE, D)
    last_rows = jnp.take_along_axis(final_rows, accepted[:, None, None], axis=1)[:, 0]
    last_state = jnp.zeros((REQUESTS, D), jnp.bfloat16).at[order].set(last_rows)
    return (layer_out, appended, last_state)
```

```python
import math

import jax
import jax.numpy as jnp
from jax import lax
from jax.sharding import PartitionSpec as P

D = 2048
HEADS = 8
HD = 128
TREE = 32


EPS = 1e-06


def scaled_norm(values, gain):
    wide = values.astype(jnp.float32)
    factor = lax.rsqrt(jnp.mean(wide * wide, axis=-1, keepdims=True) + EPS)
    return (wide * factor * gain).astype(jnp.bfloat16)


def ancestors(parent_row):
    count = parent_row.shape[0]
    index = jnp.arange(count, dtype=jnp.int32)
    links = (index[:, None] == index[None, :]) | (parent_row[:, None] == index[None, :])
    closure = links.astype(jnp.float32)
    for level in range((count - 1).bit_length()):
        closure = jnp.minimum(jnp.dot(closure, closure, precision=lax.Precision.HIGHEST), 1.0)
    return closure


def attend(block, cache_block, valid_slots, closure):
    query = block[:, :, 0]
    tree_keys = block[:, :, 1]
    tree_values = block[:, :, 2]
    slots = cache_block.shape[1]
    cache_keys = cache_block[0].reshape(slots, HEADS, HD)
    cache_values = cache_block[1].reshape(slots, HEADS, HD)
    factor = 1.0 / math.sqrt(HD)
    cache_scores = (
        jnp.einsum("thd,chd->htc", query, cache_keys, preferred_element_type=jnp.float32) * factor
    )
    position = jnp.arange(slots, dtype=jnp.int32)
    cache_scores = jnp.where(position[None, None, :] < valid_slots, cache_scores, -1e30)
    tree_scores = (
        jnp.einsum("thd,shd->hts", query, tree_keys, preferred_element_type=jnp.float32) * factor
    )
    tree_scores = jnp.where(closure[None] > 0.5, tree_scores, -1e30)
    top = jnp.maximum(jnp.max(cache_scores, axis=-1), jnp.max(tree_scores, axis=-1))[..., None]
    cache_exp = jnp.exp(cache_scores - top)
    tree_exp = jnp.exp(tree_scores - top)
    total = jnp.sum(cache_exp, axis=-1, keepdims=True) + jnp.sum(tree_exp, axis=-1, keepdims=True)
    cache_weights = (cache_exp / total).astype(jnp.bfloat16)
    tree_weights = (tree_exp / total).astype(jnp.bfloat16)
    mixed = jnp.einsum(
        "htc,chd->thd", cache_weights, cache_values, preferred_element_type=jnp.float32
    )
    mixed = mixed + jnp.einsum(
        "hts,shd->thd", tree_weights, tree_values, preferred_element_type=jnp.float32
    )
    return mixed.astype(jnp.bfloat16).reshape(block.shape[0], HEADS * HD)


def compact(closure, accepted_node, block):
    count = closure.shape[0]
    depth = jnp.sum(closure, axis=1) - 1.0
    on_path = lax.dynamic_index_in_dim(closure, accepted_node, 0, keepdims=False)
    levels = jnp.arange(count, dtype=jnp.int32).astype(jnp.float32)
    select = (on_path[None, :] * (depth[None, :] == levels[:, None]).astype(jnp.float32)).astype(
        jnp.bfloat16
    )
    tree_keys = block[:, :, 1].reshape(count, HEADS * HD)
    tree_values = block[:, :, 2].reshape(count, HEADS * HD)
    kept_keys = jnp.dot(select, tree_keys, preferred_element_type=jnp.float32).astype(jnp.bfloat16)
    kept_values = jnp.dot(select, tree_values, preferred_element_type=jnp.float32).astype(
        jnp.bfloat16
    )
    return jnp.stack([kept_keys, kept_values])


def slots_of(group_ids, experts):
    flat = group_ids.reshape(-1)
    onehot = (flat[:, None] == jnp.arange(experts, dtype=jnp.int32)[None, :]).astype(jnp.bfloat16)
    index = jnp.arange(flat.shape[0], dtype=jnp.int32)
    before = (index[None, :] < index[:, None]).astype(jnp.bfloat16)
    earlier = jnp.dot(before, onehot, preferred_element_type=jnp.float32)
    return jnp.sum(earlier * onehot.astype(jnp.float32), axis=1).astype(jnp.int32)


def expert_math(received, w_gate_up, w_down):
    gate_up = jnp.einsum(
        "gecd,ekdf->kgecf", received, w_gate_up, preferred_element_type=jnp.float32
    )
    hidden = (jax.nn.silu(gate_up[0]) * gate_up[1]).astype(jnp.bfloat16)
    return jnp.einsum("gecf,efd->gecd", hidden, w_down, preferred_element_type=jnp.float32).astype(
        jnp.bfloat16
    )


def routed_experts(moe_input, router, expert_ids, w_gate_up, w_down):
    group_input = lax.all_gather(moe_input, "fsdp", axis=0, tiled=True)
    group_rows = group_input.shape[0]
    experts = router.shape[1]
    chosen_count = expert_ids.shape[1]
    logits = jnp.dot(group_input, router, preferred_element_type=jnp.float32)
    gates = jax.nn.sigmoid(jnp.take_along_axis(logits, expert_ids, axis=1))
    slots = slots_of(expert_ids, experts)
    capacity = 2 * group_rows * chosen_count // experts
    place = expert_ids * capacity + slots.reshape(expert_ids.shape)
    hits = place[:, :, None] == jnp.arange(experts * capacity, dtype=jnp.int32)
    dispatch = jnp.any(hits, axis=1).astype(jnp.bfloat16)
    buffer = jnp.einsum(
        "ts,td->sd", dispatch, group_input, preferred_element_type=jnp.float32
    ).astype(jnp.bfloat16)
    local_experts = w_gate_up.shape[0]
    buffer = buffer.reshape(experts // local_experts, local_experts, capacity, D)
    parts = expert_math(
        lax.all_to_all(buffer, "dp", split_axis=0, concat_axis=0, tiled=True), w_gate_up, w_down
    )
    returned = lax.all_to_all(parts, "dp", split_axis=0, concat_axis=0, tiled=True)
    combine = jnp.sum(jnp.where(hits, gates[:, :, None], 0.0), axis=1)
    weighted = jnp.dot(
        combine,
        returned.reshape(experts * capacity, D).astype(jnp.float32),
        precision=lax.Precision.HIGHEST,
    )
    return lax.psum_scatter(weighted, "fsdp", scatter_dimension=0, tiled=True)


def dense_experts(moe_input, router, expert_ids, w_gate_up, w_down):
    rows = moe_input.shape[0]
    experts = router.shape[1]
    mine = lax.dynamic_slice_in_dim(expert_ids, lax.axis_index("fsdp") * rows, rows)
    logits = jnp.dot(moe_input, router, preferred_element_type=jnp.float32)
    chosen = jnp.any(mine[:, :, None] == jnp.arange(experts, dtype=jnp.int32), axis=1)
    gates = jnp.where(chosen, jax.nn.sigmoid(logits), 0.0)
    high = gates.astype(jnp.bfloat16)
    low = (gates - high.astype(jnp.float32)).astype(jnp.bfloat16)
    side = jnp.pad(jnp.concatenate([high, low], axis=1), ((0, 0), (0, 128 - 2 * experts)))
    packed = jnp.concatenate([moe_input, side], axis=1)
    everyone = lax.all_gather(packed, ("dp", "fsdp"), axis=0, tiled=True)
    tokens = everyone[:, :D]
    expert = lax.axis_index("dp")
    side = everyone[:, D:].astype(jnp.float32)
    lane = jnp.arange(128, dtype=jnp.int32)
    picked = (lane == expert) | (lane == expert + experts)
    gate = jnp.sum(jnp.where(picked[None, :], side, 0.0), axis=1, keepdims=True)
    first = jnp.dot(tokens, w_gate_up[0, 0], preferred_element_type=jnp.float32)
    second = jnp.dot(tokens, w_gate_up[0, 1], preferred_element_type=jnp.float32)
    hidden = (jax.nn.silu(first) * second).astype(jnp.bfloat16)
    part = jnp.dot(hidden, w_down[0], preferred_element_type=jnp.float32)
    part = (part * gate).astype(jnp.bfloat16)
    return lax.psum_scatter(part, ("dp", "fsdp"), scatter_dimension=0, tiled=True)


def per_device(
    drafts,
    cache,
    cache_len,
    parents,
    accepted,
    order,
    attn_gain,
    w_qkv,
    qkv_bias,
    w_out,
    moe_gain,
    router,
    expert_ids,
    w_gate_up,
    w_down,
):
    rows = drafts.shape[0]
    requests = cache.shape[0]
    feature = HEADS * HD
    group = lax.all_gather(drafts, "fsdp", axis=0, tiled=True)
    w_out, group = lax.optimization_barrier((w_out, group))
    normed = scaled_norm(group, attn_gain)
    columns = w_qkv.shape[1]
    mine = lax.axis_index("fsdp") * columns
    bias = lax.dynamic_slice_in_dim(qkv_bias, mine, columns)
    part_qkv = (jnp.dot(normed, w_qkv, preferred_element_type=jnp.float32) + bias).astype(jnp.bfloat16)
    qkv = lax.all_to_all(part_qkv, "fsdp", split_axis=0, concat_axis=1, tiled=True)
    qkv = qkv.reshape(requests, TREE, HEADS, 3, HD)

    def per_request(block, cache_block, valid_slots, parent_row, accepted_node):
        closure = ancestors(parent_row)
        return (
            attend(block, cache_block, valid_slots, closure),
            compact(closure, accepted_node, block),
        )

    attn, appended = jax.vmap(per_request)(qkv, cache, cache_len, parents, accepted)
    attn = attn.reshape(rows, feature)
    wide_out = lax.all_gather(w_out, "fsdp", axis=1, tiled=True)
    projected = jnp.dot(attn, wide_out, preferred_element_type=jnp.float32)
    resid = (drafts.astype(jnp.float32) + projected).astype(jnp.bfloat16)
    moe_input = scaled_norm(resid, moe_gain)
    if router.shape[1] <= 2 * expert_ids.shape[1] and w_gate_up.shape[0] == 1:
        moe = dense_experts(moe_input, router, expert_ids, w_gate_up, w_down)
    else:
        moe = routed_experts(moe_input, router, expert_ids, w_gate_up, w_down)
    layer_out = (resid.astype(jnp.float32) + moe.astype(jnp.float32)).astype(jnp.bfloat16)
    final_rows = layer_out.reshape(requests, TREE, D)
    last_rows = jnp.take_along_axis(final_rows, accepted[:, None, None], axis=1)[:, 0]
    everyone = lax.all_gather(last_rows, ("dp", "fsdp"), axis=0, tiled=True)
    last_state = jnp.zeros_like(everyone).at[order].set(everyone)
    return (layer_out, appended, last_state)


def solution(mesh):
    placed = (
        P(("dp", "fsdp"), None),
        P(("dp", "fsdp"), None, None, None),
        P(("dp", "fsdp")),
        P(("dp", "fsdp"), None),
        P(("dp", "fsdp")),
        P(),
        P(),
        P(None, "fsdp"),
        P(),
        P(None, "fsdp"),
        P(),
        P(),
        P("dp", None),
        P("dp", None, None, "fsdp"),
        P("dp", "fsdp", None),
    )
    return jax.shard_map(
        per_device,
        mesh=mesh,
        in_specs=placed,
        out_specs=(P(("dp", "fsdp"), None), P(("dp", "fsdp"), None, None, None), P()),
        check_vma=False,
    )
```

```python
import functools
import math

import jax
import jax.numpy as jnp
from jax import lax
from jax.experimental import pallas as pl
from jax.experimental.pallas import tpu as pltpu
from jax.sharding import PartitionSpec as P

D = 2048
HEADS = 8
HD = 128
TREE = 32


EPS = 1e-06


def scaled_norm(values, gain):
    wide = values.astype(jnp.float32)
    factor = lax.rsqrt(jnp.mean(wide * wide, axis=-1, keepdims=True) + EPS)
    return (wide * factor * gain).astype(jnp.bfloat16)


def ancestors(parent_row):
    count = parent_row.shape[0]
    index = jnp.arange(count, dtype=jnp.int32)
    links = (index[:, None] == index[None, :]) | (parent_row[:, None] == index[None, :])
    closure = links.astype(jnp.float32)
    for level in range((count - 1).bit_length()):
        closure = jnp.minimum(jnp.dot(closure, closure, precision=lax.Precision.HIGHEST), 1.0)
    return closure


def attend(block, cache_block, valid_slots, closure):
    query = block[:, :, 0]
    tree_keys = block[:, :, 1]
    tree_values = block[:, :, 2]
    slots = cache_block.shape[1]
    cache_keys = cache_block[0].reshape(slots, HEADS, HD)
    cache_values = cache_block[1].reshape(slots, HEADS, HD)
    factor = 1.0 / math.sqrt(HD)
    cache_scores = (
        jnp.einsum("thd,chd->htc", query, cache_keys, preferred_element_type=jnp.float32) * factor
    )
    position = jnp.arange(slots, dtype=jnp.int32)
    cache_scores = jnp.where(position[None, None, :] < valid_slots, cache_scores, -1e30)
    tree_scores = (
        jnp.einsum("thd,shd->hts", query, tree_keys, preferred_element_type=jnp.float32) * factor
    )
    tree_scores = jnp.where(closure[None] > 0.5, tree_scores, -1e30)
    top = jnp.maximum(jnp.max(cache_scores, axis=-1), jnp.max(tree_scores, axis=-1))[..., None]
    cache_exp = jnp.exp(cache_scores - top)
    tree_exp = jnp.exp(tree_scores - top)
    total = jnp.sum(cache_exp, axis=-1, keepdims=True) + jnp.sum(tree_exp, axis=-1, keepdims=True)
    cache_weights = (cache_exp / total).astype(jnp.bfloat16)
    tree_weights = (tree_exp / total).astype(jnp.bfloat16)
    mixed = jnp.einsum(
        "htc,chd->thd", cache_weights, cache_values, preferred_element_type=jnp.float32
    )
    mixed = mixed + jnp.einsum(
        "hts,shd->thd", tree_weights, tree_values, preferred_element_type=jnp.float32
    )
    return mixed.astype(jnp.bfloat16).reshape(block.shape[0], HEADS * HD)


def compact(closure, accepted_node, block):
    count = closure.shape[0]
    depth = jnp.sum(closure, axis=1) - 1.0
    on_path = lax.dynamic_index_in_dim(closure, accepted_node, 0, keepdims=False)
    levels = jnp.arange(count, dtype=jnp.int32).astype(jnp.float32)
    select = (on_path[None, :] * (depth[None, :] == levels[:, None]).astype(jnp.float32)).astype(
        jnp.bfloat16
    )
    tree_keys = block[:, :, 1].reshape(count, HEADS * HD)
    tree_values = block[:, :, 2].reshape(count, HEADS * HD)
    kept_keys = jnp.dot(select, tree_keys, preferred_element_type=jnp.float32).astype(jnp.bfloat16)
    kept_values = jnp.dot(select, tree_values, preferred_element_type=jnp.float32).astype(
        jnp.bfloat16
    )
    return jnp.stack([kept_keys, kept_values])


def slots_of(group_ids, experts):
    flat = group_ids.reshape(-1)
    onehot = (flat[:, None] == jnp.arange(experts, dtype=jnp.int32)[None, :]).astype(jnp.bfloat16)
    index = jnp.arange(flat.shape[0], dtype=jnp.int32)
    before = (index[None, :] < index[:, None]).astype(jnp.bfloat16)
    earlier = jnp.dot(before, onehot, preferred_element_type=jnp.float32)
    return jnp.sum(earlier * onehot.astype(jnp.float32), axis=1).astype(jnp.int32)


def expert_math(received, w_gate_up, w_down):
    gate_up = jnp.einsum(
        "gecd,ekdf->kgecf", received, w_gate_up, preferred_element_type=jnp.float32
    )
    hidden = (jax.nn.silu(gate_up[0]) * gate_up[1]).astype(jnp.bfloat16)
    return jnp.einsum("gecf,efd->gecd", hidden, w_down, preferred_element_type=jnp.float32).astype(
        jnp.bfloat16
    )


def routed_experts(moe_input, router, expert_ids, w_gate_up, w_down):
    group_input = lax.all_gather(moe_input, "fsdp", axis=0, tiled=True)
    group_rows = group_input.shape[0]
    experts = router.shape[1]
    chosen_count = expert_ids.shape[1]
    logits = jnp.dot(group_input, router, preferred_element_type=jnp.float32)
    gates = jax.nn.sigmoid(jnp.take_along_axis(logits, expert_ids, axis=1))
    slots = slots_of(expert_ids, experts)
    capacity = 2 * group_rows * chosen_count // experts
    place = expert_ids * capacity + slots.reshape(expert_ids.shape)
    hits = place[:, :, None] == jnp.arange(experts * capacity, dtype=jnp.int32)
    dispatch = jnp.any(hits, axis=1).astype(jnp.bfloat16)
    buffer = jnp.einsum(
        "ts,td->sd", dispatch, group_input, preferred_element_type=jnp.float32
    ).astype(jnp.bfloat16)
    local_experts = w_gate_up.shape[0]
    buffer = buffer.reshape(experts // local_experts, local_experts, capacity, D)
    parts = expert_math(
        lax.all_to_all(buffer, "dp", split_axis=0, concat_axis=0, tiled=True), w_gate_up, w_down
    )
    returned = lax.all_to_all(parts, "dp", split_axis=0, concat_axis=0, tiled=True)
    combine = jnp.sum(jnp.where(hits, gates[:, :, None], 0.0), axis=1)
    weighted = jnp.dot(
        combine,
        returned.reshape(experts * capacity, D).astype(jnp.float32),
        precision=lax.Precision.HIGHEST,
    )
    return lax.psum_scatter(weighted, "fsdp", scatter_dimension=0, tiled=True)


CORE, X, Y, ZHI, ZLO = range(5)


def my_bits():
    d, f = lax.axis_index("dp"), lax.axis_index("fsdp")
    return (f % 2, f // 2, d % 2, d // 4, (d // 2) % 2)


def partner(axis):
    d, f = lax.axis_index("dp"), lax.axis_index("fsdp")
    bit = my_bits()[axis]
    step = {CORE: 1, X: 2, Y: 1, ZHI: 4, ZLO: 2}[axis]
    other = step - 2 * step * bit
    return (d, f + other) if axis in (CORE, X) else (d + other, f)


def meet_partners():
    barrier = pltpu.get_barrier_semaphore()
    for axis in range(5):
        pl.semaphore_signal(
            barrier, inc=1, device_id=partner(axis), device_id_type=pl.DeviceIdType.MESH
        )
    pl.semaphore_wait(barrier, 5)


def gather_kernel(orders, columns, in_ref, out_ref, send_sem, recv_sem):
    bits = my_bits()
    out_ref[bits] = in_ref[...]
    meet_partners()
    for step in range(5):
        copies = []
        for p, order in enumerate(orders):
            done = order[:step]
            where = tuple(pl.ds(0, 2) if a in done else bits[a] for a in range(5))
            where = where + (slice(None), pl.ds(*columns[p]))
            copies.append(
                pltpu.make_async_remote_copy(
                    src_ref=out_ref.at[where],
                    dst_ref=out_ref.at[where],
                    send_sem=send_sem.at[p, step],
                    recv_sem=recv_sem.at[p, step],
                    device_id=partner(order[step]),
                    device_id_type=pl.DeviceIdType.MESH,
                )
            )
            copies[-1].start()
        for copy in copies:
            copy.wait()


def gather_blocks(block, orders, columns, number):
    shape = (2,) * 5 + block.shape
    return pl.pallas_call(
        functools.partial(gather_kernel, orders, columns),
        out_shape=jax.ShapeDtypeStruct(shape, block.dtype),
        in_specs=[pl.BlockSpec(memory_space=pltpu.VMEM)],
        out_specs=pl.BlockSpec(memory_space=pltpu.VMEM),
        scratch_shapes=[
            pltpu.SemaphoreType.DMA((len(orders), 5)),
            pltpu.SemaphoreType.DMA((len(orders), 5)),
        ],
        compiler_params=pltpu.CompilerParams(
            collective_id=number, has_side_effects=True, vmem_limit_bytes=40 * 1024 * 1024
        ),
    )(block)


def scatter_kernel(orders, columns, in_ref, out_ref, r0, r1, r2, r3, r4, send_sem, recv_sem):
    bits = my_bits()
    received = (r0, r1, r2, r3, r4)
    meet_partners()
    for step in range(5):
        copies = []
        held = in_ref if step == 0 else received[step - 1]
        for p, order in enumerate(orders):
            left = [a for a in range(5) if a not in order[:step]]
            give = tuple(1 - bits[a] if a == order[step] else pl.ds(0, 2) for a in left)
            tail = (slice(None), pl.ds(*columns[p]))
            into = tuple(pl.ds(0, 2) for _ in left[1:])
            copies.append(
                pltpu.make_async_remote_copy(
                    src_ref=held.at[give + tail],
                    dst_ref=received[step].at[into + tail],
                    send_sem=send_sem.at[p, step],
                    recv_sem=recv_sem.at[p, step],
                    device_id=partner(order[step]),
                    device_id_type=pl.DeviceIdType.MESH,
                )
            )
            copies[-1].start()
        for p, order in enumerate(orders):
            copies[p].wait()
            left = [a for a in range(5) if a not in order[:step]]
            spot = left.index(order[step])
            count = len(left) - 1
            tail = (slice(None), pl.ds(*columns[p]))

            def add(i, carry):
                index = tuple((i // 2 ** (count - 1 - k)) % 2 for k in range(count))
                mine = index[:spot] + (bits[order[step]],) + index[spot:]
                total = held[mine + tail].astype(jnp.float32) + received[step][
                    index + tail
                ].astype(jnp.float32)
                received[step][index + tail] = total.astype(jnp.bfloat16)
                return carry

            lax.fori_loop(0, 2**count, add, 0)
    out_ref[...] = received[4][...]


def scatter_sum(blocks, orders, columns, number):
    rows, width = blocks.shape[5:]
    return pl.pallas_call(
        functools.partial(scatter_kernel, orders, columns),
        out_shape=jax.ShapeDtypeStruct((rows, width), blocks.dtype),
        in_specs=[pl.BlockSpec(memory_space=pltpu.VMEM)],
        out_specs=pl.BlockSpec(memory_space=pltpu.VMEM),
        scratch_shapes=[
            pltpu.VMEM((2,) * (4 - step) + (rows, width), jnp.bfloat16) for step in range(5)
        ]
        + [
            pltpu.SemaphoreType.DMA((len(orders), 5)),
            pltpu.SemaphoreType.DMA((len(orders), 5)),
        ],
        compiler_params=pltpu.CompilerParams(
            collective_id=number, has_side_effects=True, vmem_limit_bytes=40 * 1024 * 1024
        ),
    )(blocks)


def dense_experts(moe_input, router, expert_ids, w_gate_up, w_down):
    rows = moe_input.shape[0]
    experts = router.shape[1]
    mine = lax.dynamic_slice_in_dim(expert_ids, lax.axis_index("fsdp") * rows, rows)
    logits = jnp.dot(moe_input, router, preferred_element_type=jnp.float32)
    chosen = jnp.any(mine[:, :, None] == jnp.arange(experts, dtype=jnp.int32), axis=1)
    gates = jnp.where(chosen, jax.nn.sigmoid(logits), 0.0)
    high = gates.astype(jnp.bfloat16)
    low = (gates - high.astype(jnp.float32)).astype(jnp.bfloat16)
    side = jnp.pad(jnp.concatenate([high, low], axis=1), ((0, 0), (0, 128 - 2 * experts)))
    packed = jnp.concatenate([moe_input, side], axis=1)
    orders = ((ZLO, ZHI, Y, X, CORE), (ZLO, ZHI, X, Y, CORE))
    everyone = gather_blocks(packed, orders, ((0, D // 2), (D // 2, D // 2 + 128)), 1)
    everyone = everyone.reshape(-1, D + 128)
    tokens = everyone[:, :D]
    expert = lax.axis_index("dp")
    side = everyone[:, D:].astype(jnp.float32)
    lane = jnp.arange(128, dtype=jnp.int32)
    picked = (lane == expert) | (lane == expert + experts)
    gate = jnp.sum(jnp.where(picked[None, :], side, 0.0), axis=1, keepdims=True)
    first = jnp.dot(tokens, w_gate_up[0, 0], preferred_element_type=jnp.float32)
    second = jnp.dot(tokens, w_gate_up[0, 1], preferred_element_type=jnp.float32)
    hidden = (jax.nn.silu(first) * second).astype(jnp.bfloat16)
    part = jnp.dot(hidden, w_down[0], preferred_element_type=jnp.float32)
    part = (part * gate).astype(jnp.bfloat16)
    orders = ((CORE, X, Y, ZHI, ZLO), (CORE, Y, X, ZHI, ZLO))
    blocks = part.reshape((2,) * 5 + (rows, D))
    return scatter_sum(blocks, orders, ((0, D // 2), (D // 2, D // 2)), 2)


def per_device(
    drafts,
    cache,
    cache_len,
    parents,
    accepted,
    order,
    attn_gain,
    w_qkv,
    qkv_bias,
    w_out,
    moe_gain,
    router,
    expert_ids,
    w_gate_up,
    w_down,
):
    rows = drafts.shape[0]
    requests = cache.shape[0]
    feature = HEADS * HD
    group = lax.all_gather(drafts, "fsdp", axis=0, tiled=True)
    w_out, group = lax.optimization_barrier((w_out, group))
    normed = scaled_norm(group, attn_gain)
    columns = w_qkv.shape[1]
    mine = lax.axis_index("fsdp") * columns
    bias = lax.dynamic_slice_in_dim(qkv_bias, mine, columns)
    part_qkv = (jnp.dot(normed, w_qkv, preferred_element_type=jnp.float32) + bias).astype(jnp.bfloat16)
    qkv = lax.all_to_all(part_qkv, "fsdp", split_axis=0, concat_axis=1, tiled=True)
    qkv = qkv.reshape(requests, TREE, HEADS, 3, HD)

    def per_request(block, cache_block, valid_slots, parent_row, accepted_node):
        closure = ancestors(parent_row)
        return (
            attend(block, cache_block, valid_slots, closure),
            compact(closure, accepted_node, block),
        )

    attn, appended = jax.vmap(per_request)(qkv, cache, cache_len, parents, accepted)
    attn = attn.reshape(rows, feature)
    wide_out = lax.all_gather(w_out, "fsdp", axis=1, tiled=True)
    projected = jnp.dot(attn, wide_out, preferred_element_type=jnp.float32)
    resid = (drafts.astype(jnp.float32) + projected).astype(jnp.bfloat16)
    moe_input = scaled_norm(resid, moe_gain)
    small = (lax.axis_size("dp"), lax.axis_size("fsdp")) == (8, 4)
    small = small and router.shape[1] <= 2 * expert_ids.shape[1] and w_gate_up.shape[0] == 1
    if small and requests == 1:
        moe = dense_experts(moe_input, router, expert_ids, w_gate_up, w_down)
    else:
        moe = routed_experts(moe_input, router, expert_ids, w_gate_up, w_down)
    layer_out = (resid.astype(jnp.float32) + moe.astype(jnp.float32)).astype(jnp.bfloat16)
    final_rows = layer_out.reshape(requests, TREE, D)
    last_rows = jnp.take_along_axis(final_rows, accepted[:, None, None], axis=1)[:, 0]
    if small and requests == 1:
        row = last_rows.reshape(D // 128, 128)
        everyone = gather_blocks(row, ((CORE, X, Y, ZLO, ZHI),), ((0, 128),), 3)
        everyone = everyone.transpose(3, 4, 2, 1, 0, 5, 6).reshape(-1, D)
    else:
        everyone = lax.all_gather(last_rows, ("dp", "fsdp"), axis=0, tiled=True)
    last_state = jnp.zeros_like(everyone).at[order].set(everyone)
    return (layer_out, appended, last_state)


def solution(mesh):
    placed = (
        P(("dp", "fsdp"), None),
        P(("dp", "fsdp"), None, None, None),
        P(("dp", "fsdp")),
        P(("dp", "fsdp"), None),
        P(("dp", "fsdp")),
        P(),
        P(),
        P(None, "fsdp"),
        P(),
        P(None, "fsdp"),
        P(),
        P(),
        P("dp", None),
        P("dp", None, None, "fsdp"),
        P("dp", "fsdp", None),
    )
    return jax.shard_map(
        per_device,
        mesh=mesh,
        in_specs=placed,
        out_specs=(P(("dp", "fsdp"), None), P(("dp", "fsdp"), None, None, None), P()),
        check_vma=False,
    )
```

```python
import functools
import math

import jax
import jax.numpy as jnp
from jax import lax
from jax.experimental import pallas as pl
from jax.experimental.pallas import tpu as pltpu
from jax.sharding import PartitionSpec as P

D = 2048
HEADS = 8
HD = 128
TREE = 32


EPS = 1e-06


def scaled_norm(values, gain):
    wide = values.astype(jnp.float32)
    factor = lax.rsqrt(jnp.mean(wide * wide, axis=-1, keepdims=True) + EPS)
    return (wide * factor * gain).astype(jnp.bfloat16)


def ancestors(parent_row):
    count = parent_row.shape[0]
    index = jnp.arange(count, dtype=jnp.int32)
    links = (index[:, None] == index[None, :]) | (parent_row[:, None] == index[None, :])
    closure = links.astype(jnp.float32)
    for level in range((count - 1).bit_length()):
        closure = jnp.minimum(jnp.dot(closure, closure, precision=lax.Precision.HIGHEST), 1.0)
    return closure


def attend(block, cache_block, valid_slots, closure):
    query = block[:, :, 0]
    tree_keys = block[:, :, 1]
    tree_values = block[:, :, 2]
    slots = cache_block.shape[1]
    cache_keys = cache_block[0].reshape(slots, HEADS, HD)
    cache_values = cache_block[1].reshape(slots, HEADS, HD)
    factor = 1.0 / math.sqrt(HD)
    cache_scores = (
        jnp.einsum("thd,chd->htc", query, cache_keys, preferred_element_type=jnp.float32) * factor
    )
    position = jnp.arange(slots, dtype=jnp.int32)
    cache_scores = jnp.where(position[None, None, :] < valid_slots, cache_scores, -1e30)
    tree_scores = (
        jnp.einsum("thd,shd->hts", query, tree_keys, preferred_element_type=jnp.float32) * factor
    )
    tree_scores = jnp.where(closure[None] > 0.5, tree_scores, -1e30)
    top = jnp.maximum(jnp.max(cache_scores, axis=-1), jnp.max(tree_scores, axis=-1))[..., None]
    cache_exp = jnp.exp(cache_scores - top)
    tree_exp = jnp.exp(tree_scores - top)
    total = jnp.sum(cache_exp, axis=-1, keepdims=True) + jnp.sum(tree_exp, axis=-1, keepdims=True)
    cache_weights = (cache_exp / total).astype(jnp.bfloat16)
    tree_weights = (tree_exp / total).astype(jnp.bfloat16)
    mixed = jnp.einsum(
        "htc,chd->thd", cache_weights, cache_values, preferred_element_type=jnp.float32
    )
    mixed = mixed + jnp.einsum(
        "hts,shd->thd", tree_weights, tree_values, preferred_element_type=jnp.float32
    )
    return mixed.astype(jnp.bfloat16).reshape(block.shape[0], HEADS * HD)


def compact(closure, accepted_node, block):
    count = closure.shape[0]
    depth = jnp.sum(closure, axis=1) - 1.0
    on_path = lax.dynamic_index_in_dim(closure, accepted_node, 0, keepdims=False)
    levels = jnp.arange(count, dtype=jnp.int32).astype(jnp.float32)
    select = (on_path[None, :] * (depth[None, :] == levels[:, None]).astype(jnp.float32)).astype(
        jnp.bfloat16
    )
    tree_keys = block[:, :, 1].reshape(count, HEADS * HD)
    tree_values = block[:, :, 2].reshape(count, HEADS * HD)
    kept_keys = jnp.dot(select, tree_keys, preferred_element_type=jnp.float32).astype(jnp.bfloat16)
    kept_values = jnp.dot(select, tree_values, preferred_element_type=jnp.float32).astype(
        jnp.bfloat16
    )
    return jnp.stack([kept_keys, kept_values])


def slots_of(group_ids, experts):
    flat = group_ids.reshape(-1)
    onehot = (flat[:, None] == jnp.arange(experts, dtype=jnp.int32)[None, :]).astype(jnp.bfloat16)
    index = jnp.arange(flat.shape[0], dtype=jnp.int32)
    before = (index[None, :] < index[:, None]).astype(jnp.bfloat16)
    earlier = jnp.dot(before, onehot, preferred_element_type=jnp.float32)
    return jnp.sum(earlier * onehot.astype(jnp.float32), axis=1).astype(jnp.int32)


def expert_math(received, w_gate_up, w_down):
    gate_up = jnp.einsum(
        "gecd,ekdf->kgecf", received, w_gate_up, preferred_element_type=jnp.float32
    )
    hidden = (jax.nn.silu(gate_up[0]) * gate_up[1]).astype(jnp.bfloat16)
    return jnp.einsum("gecf,efd->gecd", hidden, w_down, preferred_element_type=jnp.float32).astype(
        jnp.bfloat16
    )


def routed_experts(moe_input, router, expert_ids, w_gate_up, w_down):
    group_input = lax.all_gather(moe_input, "fsdp", axis=0, tiled=True)
    group_rows = group_input.shape[0]
    experts = router.shape[1]
    chosen_count = expert_ids.shape[1]
    logits = jnp.dot(group_input, router, preferred_element_type=jnp.float32)
    gates = jax.nn.sigmoid(jnp.take_along_axis(logits, expert_ids, axis=1))
    slots = slots_of(expert_ids, experts)
    capacity = 2 * group_rows * chosen_count // experts
    place = expert_ids * capacity + slots.reshape(expert_ids.shape)
    hits = place[:, :, None] == jnp.arange(experts * capacity, dtype=jnp.int32)
    dispatch = jnp.any(hits, axis=1).astype(jnp.bfloat16)
    buffer = jnp.einsum(
        "ts,td->sd", dispatch, group_input, preferred_element_type=jnp.float32
    ).astype(jnp.bfloat16)
    local_experts = w_gate_up.shape[0]
    buffer = buffer.reshape(experts // local_experts, local_experts, capacity, D)
    parts = expert_math(
        lax.all_to_all(buffer, "dp", split_axis=0, concat_axis=0, tiled=True), w_gate_up, w_down
    )
    returned = lax.all_to_all(parts, "dp", split_axis=0, concat_axis=0, tiled=True)
    combine = jnp.sum(jnp.where(hits, gates[:, :, None], 0.0), axis=1)
    weighted = jnp.dot(
        combine,
        returned.reshape(experts * capacity, D).astype(jnp.float32),
        precision=lax.Precision.HIGHEST,
    )
    return lax.psum_scatter(weighted, "fsdp", scatter_dimension=0, tiled=True)


CORE, X, Y, ZHI, ZLO = range(5)


def my_bits():
    d, f = lax.axis_index("dp"), lax.axis_index("fsdp")
    return (f % 2, f // 2, d % 2, d // 4, (d // 2) % 2)


def partner(axis):
    d, f = lax.axis_index("dp"), lax.axis_index("fsdp")
    bit = my_bits()[axis]
    step = {CORE: 1, X: 2, Y: 1, ZHI: 4, ZLO: 2}[axis]
    other = step - 2 * step * bit
    return (d, f + other) if axis in (CORE, X) else (d + other, f)


def meet_partners():
    barrier = pltpu.get_barrier_semaphore()
    for axis in range(5):
        pl.semaphore_signal(
            barrier, inc=1, device_id=partner(axis), device_id_type=pl.DeviceIdType.MESH
        )
    pl.semaphore_wait(barrier, 5)


def gather_kernel(orders, columns, in_ref, out_ref, send_sem, recv_sem):
    bits = my_bits()
    out_ref[bits] = in_ref[...]
    meet_partners()
    flying = [None] * len(orders)
    for step in range(5):
        for p, order in enumerate(orders):
            if flying[p] is not None:
                flying[p].wait()
            done = order[:step]
            where = tuple(pl.ds(0, 2) if a in done else bits[a] for a in range(5))
            where = where + (slice(None), pl.ds(*columns[p]))
            flying[p] = pltpu.make_async_remote_copy(
                src_ref=out_ref.at[where],
                dst_ref=out_ref.at[where],
                send_sem=send_sem.at[p, step],
                recv_sem=recv_sem.at[p, step],
                device_id=partner(order[step]),
                device_id_type=pl.DeviceIdType.MESH,
            )
            flying[p].start()
    for copy in flying:
        copy.wait()


def gather_blocks(block, orders, columns, number):
    shape = (2,) * 5 + block.shape
    return pl.pallas_call(
        functools.partial(gather_kernel, orders, columns),
        out_shape=jax.ShapeDtypeStruct(shape, block.dtype),
        in_specs=[pl.BlockSpec(memory_space=pltpu.VMEM)],
        out_specs=pl.BlockSpec(memory_space=pltpu.VMEM),
        scratch_shapes=[
            pltpu.SemaphoreType.DMA((len(orders), 5)),
            pltpu.SemaphoreType.DMA((len(orders), 5)),
        ],
        compiler_params=pltpu.CompilerParams(
            collective_id=number, has_side_effects=True, vmem_limit_bytes=40 * 1024 * 1024
        ),
    )(block)


def scatter_kernel(orders, columns, in_ref, out_ref, r0, r1, r2, r3, r4, send_sem, recv_sem):
    bits = my_bits()
    received = (r0, r1, r2, r3, r4)
    meet_partners()
    flying = [None] * len(orders)

    def take_in(p, step):
        order = orders[p]
        held = in_ref if step == 0 else received[step - 1]
        left = [a for a in range(5) if a not in order[:step]]
        spot = left.index(order[step])
        count = len(left) - 1
        tail = (slice(None), pl.ds(*columns[p]))
        flying[p].wait()

        def add(i, carry):
            index = tuple((i // 2 ** (count - 1 - k)) % 2 for k in range(count))
            mine = index[:spot] + (bits[order[step]],) + index[spot:]
            total = held[mine + tail].astype(jnp.float32) + received[step][
                index + tail
            ].astype(jnp.float32)
            received[step][index + tail] = total.astype(jnp.bfloat16)
            return carry

        lax.fori_loop(0, 2**count, add, 0)

    for step in range(5):
        held = in_ref if step == 0 else received[step - 1]
        for p, order in enumerate(orders):
            if step > 0:
                take_in(p, step - 1)
            left = [a for a in range(5) if a not in order[:step]]
            give = tuple(1 - bits[a] if a == order[step] else pl.ds(0, 2) for a in left)
            tail = (slice(None), pl.ds(*columns[p]))
            into = tuple(pl.ds(0, 2) for _ in left[1:])
            flying[p] = pltpu.make_async_remote_copy(
                src_ref=held.at[give + tail],
                dst_ref=received[step].at[into + tail],
                send_sem=send_sem.at[p, step],
                recv_sem=recv_sem.at[p, step],
                device_id=partner(order[step]),
                device_id_type=pl.DeviceIdType.MESH,
            )
            flying[p].start()
    for p in range(len(orders)):
        take_in(p, 4)
    out_ref[...] = received[4][...]


def scatter_sum(blocks, orders, columns, number):
    rows, width = blocks.shape[5:]
    return pl.pallas_call(
        functools.partial(scatter_kernel, orders, columns),
        out_shape=jax.ShapeDtypeStruct((rows, width), blocks.dtype),
        in_specs=[pl.BlockSpec(memory_space=pltpu.VMEM)],
        out_specs=pl.BlockSpec(memory_space=pltpu.VMEM),
        scratch_shapes=[
            pltpu.VMEM((2,) * (4 - step) + (rows, width), jnp.bfloat16) for step in range(5)
        ]
        + [
            pltpu.SemaphoreType.DMA((len(orders), 5)),
            pltpu.SemaphoreType.DMA((len(orders), 5)),
        ],
        compiler_params=pltpu.CompilerParams(
            collective_id=number, has_side_effects=True, vmem_limit_bytes=40 * 1024 * 1024
        ),
    )(blocks)


def dense_experts(moe_input, router, expert_ids, w_gate_up, w_down):
    rows = moe_input.shape[0]
    experts = router.shape[1]
    mine = lax.dynamic_slice_in_dim(expert_ids, lax.axis_index("fsdp") * rows, rows)
    logits = jnp.dot(moe_input, router, preferred_element_type=jnp.float32)
    chosen = jnp.any(mine[:, :, None] == jnp.arange(experts, dtype=jnp.int32), axis=1)
    gates = jnp.where(chosen, jax.nn.sigmoid(logits), 0.0)
    high = gates.astype(jnp.bfloat16)
    low = (gates - high.astype(jnp.float32)).astype(jnp.bfloat16)
    side = jnp.pad(jnp.concatenate([high, low], axis=1), ((0, 0), (0, 128 - 2 * experts)))
    packed = jnp.concatenate([moe_input, side], axis=1)
    orders = ((ZHI, ZLO, Y, X, CORE), (ZHI, ZLO, X, Y, CORE)) * 2
    quarter = D // 4
    columns = tuple((p * quarter, quarter + (128 if p == 3 else 0)) for p in range(4))
    everyone = gather_blocks(packed, orders, columns, 1)
    everyone = everyone.reshape(-1, D + 128)
    tokens = everyone[:, :D]
    expert = lax.axis_index("dp")
    side = everyone[:, D:].astype(jnp.float32)
    lane = jnp.arange(128, dtype=jnp.int32)
    picked = (lane == expert) | (lane == expert + experts)
    gate = jnp.sum(jnp.where(picked[None, :], side, 0.0), axis=1, keepdims=True)
    first = jnp.dot(tokens, w_gate_up[0, 0], preferred_element_type=jnp.float32)
    second = jnp.dot(tokens, w_gate_up[0, 1], preferred_element_type=jnp.float32)
    hidden = (jax.nn.silu(first) * second).astype(jnp.bfloat16)
    part = jnp.dot(hidden, w_down[0], preferred_element_type=jnp.float32)
    part = (part * gate).astype(jnp.bfloat16)
    orders = ((CORE, X, Y, ZLO, ZHI), (CORE, Y, X, ZLO, ZHI)) * 2
    columns = tuple((p * quarter, quarter) for p in range(4))
    blocks = part.reshape((2,) * 5 + (rows, D))
    return scatter_sum(blocks, orders, columns, 2)


def per_device(
    drafts,
    cache,
    cache_len,
    parents,
    accepted,
    order,
    attn_gain,
    w_qkv,
    qkv_bias,
    w_out,
    moe_gain,
    router,
    expert_ids,
    w_gate_up,
    w_down,
):
    rows = drafts.shape[0]
    requests = cache.shape[0]
    feature = HEADS * HD
    group = lax.all_gather(drafts, "fsdp", axis=0, tiled=True)
    w_out, group = lax.optimization_barrier((w_out, group))
    normed = scaled_norm(group, attn_gain)
    columns = w_qkv.shape[1]
    mine = lax.axis_index("fsdp") * columns
    bias = lax.dynamic_slice_in_dim(qkv_bias, mine, columns)
    part_qkv = (jnp.dot(normed, w_qkv, preferred_element_type=jnp.float32) + bias).astype(jnp.bfloat16)
    qkv = lax.all_to_all(part_qkv, "fsdp", split_axis=0, concat_axis=1, tiled=True)
    qkv = qkv.reshape(requests, TREE, HEADS, 3, HD)

    def per_request(block, cache_block, valid_slots, parent_row, accepted_node):
        closure = ancestors(parent_row)
        return (
            attend(block, cache_block, valid_slots, closure),
            compact(closure, accepted_node, block),
        )

    attn, appended = jax.vmap(per_request)(qkv, cache, cache_len, parents, accepted)
    attn = attn.reshape(rows, feature)
    wide_out = lax.all_gather(w_out, "fsdp", axis=1, tiled=True)
    projected = jnp.dot(attn, wide_out, preferred_element_type=jnp.float32)
    resid = (drafts.astype(jnp.float32) + projected).astype(jnp.bfloat16)
    moe_input = scaled_norm(resid, moe_gain)
    small = (lax.axis_size("dp"), lax.axis_size("fsdp")) == (8, 4)
    small = small and router.shape[1] <= 2 * expert_ids.shape[1] and w_gate_up.shape[0] == 1
    if small and requests == 1:
        moe = dense_experts(moe_input, router, expert_ids, w_gate_up, w_down)
    else:
        moe = routed_experts(moe_input, router, expert_ids, w_gate_up, w_down)
    layer_out = (resid.astype(jnp.float32) + moe.astype(jnp.float32)).astype(jnp.bfloat16)
    final_rows = layer_out.reshape(requests, TREE, D)
    last_rows = jnp.take_along_axis(final_rows, accepted[:, None, None], axis=1)[:, 0]
    if small and requests == 1:
        row = last_rows.reshape(D // 128, 128)
        everyone = gather_blocks(row, ((CORE, X, Y, ZLO, ZHI),), ((0, 128),), 3)
        everyone = everyone.transpose(3, 4, 2, 1, 0, 5, 6).reshape(-1, D)
    else:
        everyone = lax.all_gather(last_rows, ("dp", "fsdp"), axis=0, tiled=True)
    last_state = jnp.zeros_like(everyone).at[order].set(everyone)
    return (layer_out, appended, last_state)


def solution(mesh):
    placed = (
        P(("dp", "fsdp"), None),
        P(("dp", "fsdp"), None, None, None),
        P(("dp", "fsdp")),
        P(("dp", "fsdp"), None),
        P(("dp", "fsdp")),
        P(),
        P(),
        P(None, "fsdp"),
        P(),
        P(None, "fsdp"),
        P(),
        P(),
        P("dp", None),
        P("dp", None, None, "fsdp"),
        P("dp", "fsdp", None),
    )
    return jax.shard_map(
        per_device,
        mesh=mesh,
        in_specs=placed,
        out_specs=(P(("dp", "fsdp"), None), P(("dp", "fsdp"), None, None, None), P()),
        check_vma=False,
    )
```

```python
import functools
import math

import jax
import jax.numpy as jnp
from jax import lax
from jax.experimental import pallas as pl
from jax.experimental.pallas import tpu as pltpu
from jax.sharding import PartitionSpec as P

D = 2048
HEADS = 8
HD = 128
TREE = 32


EPS = 1e-06


def scaled_norm(values, gain):
    wide = values.astype(jnp.float32)
    factor = lax.rsqrt(jnp.mean(wide * wide, axis=-1, keepdims=True) + EPS)
    return (wide * factor * gain).astype(jnp.bfloat16)


def ancestors(parent_row):
    count = parent_row.shape[0]
    index = jnp.arange(count, dtype=jnp.int32)
    links = (index[:, None] == index[None, :]) | (parent_row[:, None] == index[None, :])
    closure = links.astype(jnp.float32)
    for level in range((count - 1).bit_length()):
        closure = jnp.minimum(jnp.dot(closure, closure, precision=lax.Precision.HIGHEST), 1.0)
    return closure


def attend(block, cache_block, valid_slots, closure):
    query = block[:, :, 0]
    tree_keys = block[:, :, 1]
    tree_values = block[:, :, 2]
    slots = cache_block.shape[1]
    cache_keys = cache_block[0].reshape(slots, HEADS, HD)
    cache_values = cache_block[1].reshape(slots, HEADS, HD)
    factor = 1.0 / math.sqrt(HD)
    cache_scores = (
        jnp.einsum("thd,chd->htc", query, cache_keys, preferred_element_type=jnp.float32) * factor
    )
    position = jnp.arange(slots, dtype=jnp.int32)
    cache_scores = jnp.where(position[None, None, :] < valid_slots, cache_scores, -1e30)
    tree_scores = (
        jnp.einsum("thd,shd->hts", query, tree_keys, preferred_element_type=jnp.float32) * factor
    )
    tree_scores = jnp.where(closure[None] > 0.5, tree_scores, -1e30)
    top = jnp.maximum(jnp.max(cache_scores, axis=-1), jnp.max(tree_scores, axis=-1))[..., None]
    cache_exp = jnp.exp(cache_scores - top)
    tree_exp = jnp.exp(tree_scores - top)
    total = jnp.sum(cache_exp, axis=-1, keepdims=True) + jnp.sum(tree_exp, axis=-1, keepdims=True)
    cache_weights = (cache_exp / total).astype(jnp.bfloat16)
    tree_weights = (tree_exp / total).astype(jnp.bfloat16)
    mixed = jnp.einsum(
        "htc,chd->thd", cache_weights, cache_values, preferred_element_type=jnp.float32
    )
    mixed = mixed + jnp.einsum(
        "hts,shd->thd", tree_weights, tree_values, preferred_element_type=jnp.float32
    )
    return mixed.astype(jnp.bfloat16).reshape(block.shape[0], HEADS * HD)


def compact(closure, accepted_node, block):
    count = closure.shape[0]
    depth = jnp.sum(closure, axis=1) - 1.0
    on_path = lax.dynamic_index_in_dim(closure, accepted_node, 0, keepdims=False)
    levels = jnp.arange(count, dtype=jnp.int32).astype(jnp.float32)
    select = (on_path[None, :] * (depth[None, :] == levels[:, None]).astype(jnp.float32)).astype(
        jnp.bfloat16
    )
    tree_keys = block[:, :, 1].reshape(count, HEADS * HD)
    tree_values = block[:, :, 2].reshape(count, HEADS * HD)
    kept_keys = jnp.dot(select, tree_keys, preferred_element_type=jnp.float32).astype(jnp.bfloat16)
    kept_values = jnp.dot(select, tree_values, preferred_element_type=jnp.float32).astype(
        jnp.bfloat16
    )
    return jnp.stack([kept_keys, kept_values])


def slots_of(group_ids, experts):
    flat = group_ids.reshape(-1)
    onehot = (flat[:, None] == jnp.arange(experts, dtype=jnp.int32)[None, :]).astype(jnp.bfloat16)
    index = jnp.arange(flat.shape[0], dtype=jnp.int32)
    before = (index[None, :] < index[:, None]).astype(jnp.bfloat16)
    earlier = jnp.dot(before, onehot, preferred_element_type=jnp.float32)
    return jnp.sum(earlier * onehot.astype(jnp.float32), axis=1).astype(jnp.int32)


def expert_math(received, w_gate_up, w_down):
    gate_up = jnp.einsum(
        "gecd,ekdf->kgecf", received, w_gate_up, preferred_element_type=jnp.float32
    )
    hidden = (jax.nn.silu(gate_up[0]) * gate_up[1]).astype(jnp.bfloat16)
    return jnp.einsum("gecf,efd->gecd", hidden, w_down, preferred_element_type=jnp.float32).astype(
        jnp.bfloat16
    )


def routed_experts(moe_input, router, expert_ids, w_gate_up, w_down):
    group_input = lax.all_gather(moe_input, "fsdp", axis=0, tiled=True)
    group_rows = group_input.shape[0]
    experts = router.shape[1]
    chosen_count = expert_ids.shape[1]
    logits = jnp.dot(group_input, router, preferred_element_type=jnp.float32)
    gates = jax.nn.sigmoid(jnp.take_along_axis(logits, expert_ids, axis=1))
    slots = slots_of(expert_ids, experts)
    capacity = 2 * group_rows * chosen_count // experts
    place = expert_ids * capacity + slots.reshape(expert_ids.shape)
    hits = place[:, :, None] == jnp.arange(experts * capacity, dtype=jnp.int32)
    dispatch = jnp.any(hits, axis=1).astype(jnp.bfloat16)
    buffer = jnp.einsum(
        "ts,td->sd", dispatch, group_input, preferred_element_type=jnp.float32
    ).astype(jnp.bfloat16)
    local_experts = w_gate_up.shape[0]
    buffer = buffer.reshape(experts // local_experts, local_experts, capacity, D)
    parts = expert_math(
        lax.all_to_all(buffer, "dp", split_axis=0, concat_axis=0, tiled=True), w_gate_up, w_down
    )
    returned = lax.all_to_all(parts, "dp", split_axis=0, concat_axis=0, tiled=True)
    combine = jnp.sum(jnp.where(hits, gates[:, :, None], 0.0), axis=1)
    weighted = jnp.dot(
        combine,
        returned.reshape(experts * capacity, D).astype(jnp.float32),
        precision=lax.Precision.HIGHEST,
    )
    return lax.psum_scatter(weighted, "fsdp", scatter_dimension=0, tiled=True)


CORE, X, Y, ZHI, ZLO = range(5)


def my_bits():
    d, f = lax.axis_index("dp"), lax.axis_index("fsdp")
    return (f % 2, f // 2, d % 2, d // 4, (d // 2) % 2)


def partner(axis):
    d, f = lax.axis_index("dp"), lax.axis_index("fsdp")
    bit = my_bits()[axis]
    step = {CORE: 1, X: 2, Y: 1, ZHI: 4, ZLO: 2}[axis]
    other = step - 2 * step * bit
    return (d, f + other) if axis in (CORE, X) else (d + other, f)


def meet_partners():
    barrier = pltpu.get_barrier_semaphore()
    for axis in range(5):
        pl.semaphore_signal(
            barrier, inc=1, device_id=partner(axis), device_id_type=pl.DeviceIdType.MESH
        )
    pl.semaphore_wait(barrier, 5)


def gather_kernel(orders, columns, in_ref, out_ref, send_sem, recv_sem):
    bits = my_bits()
    out_ref[bits] = in_ref[...]
    meet_partners()
    flying = [None] * len(orders)
    for step in range(5):
        for p, order in enumerate(orders):
            if flying[p] is not None:
                flying[p].wait()
            done = order[:step]
            where = tuple(pl.ds(0, 2) if a in done else bits[a] for a in range(5))
            where = where + (slice(None), pl.ds(*columns[p]))
            flying[p] = pltpu.make_async_remote_copy(
                src_ref=out_ref.at[where],
                dst_ref=out_ref.at[where],
                send_sem=send_sem.at[p, step],
                recv_sem=recv_sem.at[p, step],
                device_id=partner(order[step]),
                device_id_type=pl.DeviceIdType.MESH,
            )
            flying[p].start()
    for copy in flying:
        copy.wait()


def gather_blocks(block, orders, columns, number):
    shape = (2,) * 5 + block.shape
    return pl.pallas_call(
        functools.partial(gather_kernel, orders, columns),
        out_shape=jax.ShapeDtypeStruct(shape, block.dtype),
        in_specs=[pl.BlockSpec(memory_space=pltpu.VMEM)],
        out_specs=pl.BlockSpec(memory_space=pltpu.VMEM),
        scratch_shapes=[
            pltpu.SemaphoreType.DMA((len(orders), 5)),
            pltpu.SemaphoreType.DMA((len(orders), 5)),
        ],
        compiler_params=pltpu.CompilerParams(
            collective_id=number, has_side_effects=True, vmem_limit_bytes=40 * 1024 * 1024
        ),
    )(block)


def scatter_kernel(orders, columns, in_ref, out_ref, r0, r1, r2, r3, r4, send_sem, recv_sem):
    bits = my_bits()
    received = (r0, r1, r2, r3, r4)
    meet_partners()
    flying = [None] * len(orders)

    def take_in(p, step):
        order = orders[p]
        held = in_ref if step == 0 else received[step - 1]
        left = [a for a in range(5) if a not in order[:step]]
        spot = left.index(order[step])
        count = len(left) - 1
        tail = (slice(None), pl.ds(*columns[p]))
        flying[p].wait()

        def add(i, carry):
            index = tuple((i // 2 ** (count - 1 - k)) % 2 for k in range(count))
            mine = index[:spot] + (bits[order[step]],) + index[spot:]
            total = held[mine + tail].astype(jnp.float32) + received[step][
                index + tail
            ].astype(jnp.float32)
            received[step][index + tail] = total.astype(jnp.bfloat16)
            return carry

        lax.fori_loop(0, 2**count, add, 0)

    for step in range(5):
        held = in_ref if step == 0 else received[step - 1]
        for p, order in enumerate(orders):
            if step > 0:
                take_in(p, step - 1)
            left = [a for a in range(5) if a not in order[:step]]
            give = tuple(1 - bits[a] if a == order[step] else pl.ds(0, 2) for a in left)
            tail = (slice(None), pl.ds(*columns[p]))
            into = tuple(pl.ds(0, 2) for _ in left[1:])
            flying[p] = pltpu.make_async_remote_copy(
                src_ref=held.at[give + tail],
                dst_ref=received[step].at[into + tail],
                send_sem=send_sem.at[p, step],
                recv_sem=recv_sem.at[p, step],
                device_id=partner(order[step]),
                device_id_type=pl.DeviceIdType.MESH,
            )
            flying[p].start()
    for p in range(len(orders)):
        take_in(p, 4)
    out_ref[...] = received[4][...]


def scatter_sum(blocks, orders, columns, number):
    rows, width = blocks.shape[5:]
    return pl.pallas_call(
        functools.partial(scatter_kernel, orders, columns),
        out_shape=jax.ShapeDtypeStruct((rows, width), blocks.dtype),
        in_specs=[pl.BlockSpec(memory_space=pltpu.VMEM)],
        out_specs=pl.BlockSpec(memory_space=pltpu.VMEM),
        scratch_shapes=[
            pltpu.VMEM((2,) * (4 - step) + (rows, width), jnp.bfloat16) for step in range(5)
        ]
        + [
            pltpu.SemaphoreType.DMA((len(orders), 5)),
            pltpu.SemaphoreType.DMA((len(orders), 5)),
        ],
        compiler_params=pltpu.CompilerParams(
            collective_id=number, has_side_effects=True, vmem_limit_bytes=40 * 1024 * 1024
        ),
    )(blocks)


def dense_experts(moe_input, router, expert_ids, w_gate_up, w_down):
    rows = moe_input.shape[0]
    experts = router.shape[1]
    mine = lax.dynamic_slice_in_dim(expert_ids, lax.axis_index("fsdp") * rows, rows)
    logits = jnp.dot(moe_input, router, preferred_element_type=jnp.float32)
    chosen = jnp.any(mine[:, :, None] == jnp.arange(experts, dtype=jnp.int32), axis=1)
    gates = jnp.where(chosen, jax.nn.sigmoid(logits), 0.0)
    high = gates.astype(jnp.bfloat16)
    low = (gates - high.astype(jnp.float32)).astype(jnp.bfloat16)
    side = jnp.pad(jnp.concatenate([high, low], axis=1), ((0, 0), (0, 128 - 2 * experts)))
    packed = jnp.concatenate([moe_input, side], axis=1)
    orders = ((ZHI, ZLO, Y, X, CORE), (ZHI, ZLO, X, Y, CORE)) * 2
    quarter = D // 4
    columns = tuple((p * quarter, quarter + (128 if p == 3 else 0)) for p in range(4))
    everyone = gather_blocks(packed, orders, columns, 1)
    everyone = everyone.reshape(-1, D + 128)
    tokens = everyone[:, :D]
    expert = lax.axis_index("dp")
    side = everyone[:, D:].astype(jnp.float32)
    lane = jnp.arange(128, dtype=jnp.int32)
    picked = (lane == expert) | (lane == expert + experts)
    gate = jnp.sum(jnp.where(picked[None, :], side, 0.0), axis=1, keepdims=True)
    first = jnp.dot(tokens, w_gate_up[0, 0], preferred_element_type=jnp.float32)
    second = jnp.dot(tokens, w_gate_up[0, 1], preferred_element_type=jnp.float32)
    hidden = (jax.nn.silu(first) * second).astype(jnp.bfloat16)
    part = jnp.dot(hidden, w_down[0], preferred_element_type=jnp.float32)
    part = (part * gate).astype(jnp.bfloat16)
    orders = ((CORE, X, Y, ZLO, ZHI), (CORE, Y, X, ZLO, ZHI)) * 2
    columns = tuple((p * quarter, quarter) for p in range(4))
    blocks = part.reshape((2,) * 5 + (rows, D))
    return scatter_sum(blocks, orders, columns, 2)


def per_device(
    drafts,
    cache,
    cache_len,
    parents,
    accepted,
    order,
    attn_gain,
    w_qkv,
    qkv_bias,
    w_out,
    moe_gain,
    router,
    expert_ids,
    w_gate_up,
    w_down,
):
    rows = drafts.shape[0]
    requests = cache.shape[0]
    feature = HEADS * HD
    group = lax.all_gather(drafts, "fsdp", axis=0, tiled=True)
    normed = scaled_norm(group, attn_gain)
    columns = w_qkv.shape[1]
    mine = lax.axis_index("fsdp") * columns
    bias = lax.dynamic_slice_in_dim(qkv_bias, mine, columns)
    part_qkv = (jnp.dot(normed, w_qkv, preferred_element_type=jnp.float32) + bias).astype(jnp.bfloat16)
    qkv = lax.all_to_all(part_qkv, "fsdp", split_axis=0, concat_axis=1, tiled=True)
    qkv = qkv.reshape(requests, TREE, HEADS, 3, HD)

    def per_request(block, cache_block, valid_slots, parent_row, accepted_node):
        closure = ancestors(parent_row)
        return (
            attend(block, cache_block, valid_slots, closure),
            compact(closure, accepted_node, block),
        )

    attn, appended = jax.vmap(per_request)(qkv, cache, cache_len, parents, accepted)
    attn = attn.reshape(rows, feature)
    wide_out = lax.all_gather(w_out, "fsdp", axis=1, tiled=True)
    projected = jnp.dot(attn, wide_out, preferred_element_type=jnp.float32)
    resid = (drafts.astype(jnp.float32) + projected).astype(jnp.bfloat16)
    moe_input = scaled_norm(resid, moe_gain)
    small = (lax.axis_size("dp"), lax.axis_size("fsdp")) == (8, 4)
    small = small and router.shape[1] <= 2 * expert_ids.shape[1] and w_gate_up.shape[0] == 1
    if small and requests == 1:
        moe = dense_experts(moe_input, router, expert_ids, w_gate_up, w_down)
    else:
        moe = routed_experts(moe_input, router, expert_ids, w_gate_up, w_down)
    layer_out = (resid.astype(jnp.float32) + moe.astype(jnp.float32)).astype(jnp.bfloat16)
    final_rows = layer_out.reshape(requests, TREE, D)
    last_rows = jnp.take_along_axis(final_rows, accepted[:, None, None], axis=1)[:, 0]
    if small and requests == 1:
        row = last_rows.reshape(D // 128, 128)
        everyone = gather_blocks(row, ((CORE, X, Y, ZLO, ZHI),), ((0, 128),), 3)
        everyone = everyone.transpose(3, 4, 2, 1, 0, 5, 6).reshape(-1, D)
    else:
        everyone = lax.all_gather(last_rows, ("dp", "fsdp"), axis=0, tiled=True)
    last_state = jnp.zeros_like(everyone).at[order].set(everyone)
    return (layer_out, appended, last_state)


def solution(mesh):
    placed = (
        P(("dp", "fsdp"), None),
        P(("dp", "fsdp"), None, None, None),
        P(("dp", "fsdp")),
        P(("dp", "fsdp"), None),
        P(("dp", "fsdp")),
        P(),
        P(),
        P(None, "fsdp"),
        P(),
        P(None, "fsdp"),
        P(),
        P(),
        P("dp", None),
        P("dp", None, None, "fsdp"),
        P("dp", "fsdp", None),
    )
    return jax.shard_map(
        per_device,
        mesh=mesh,
        in_specs=placed,
        out_specs=(P(("dp", "fsdp"), None), P(("dp", "fsdp"), None, None, None), P()),
        check_vma=False,
    )
```
